512 devices in a mesh: row: 32 (over y, z_lo, core), col: 16 (over z_hi, x).
Axes of the slice: x: 4, y: 4, z: 16 (z_hi: 4, z_lo: 4; z = z_hi * 4 + z_lo), core: 2. Of those that a mesh axis runs over, the one named last changes fastest.
Arguments:
- activations: bfloat16 [1024, 14848], P('col', 'row'), may hold values from -6 to 6
- output_grads: bfloat16 [1024, 29696], P('row', 'col'), may hold values from -1 to 1
- weight: bfloat16 [14848, 29696], P('row', 'col'), may hold values from -0.046875 to 0.046875
- step_sizes: float32 [29696], P('col'), may hold values from 0.00012207031 to 0.001953125, as said below
- level_low: int32 [1], replicated, may hold values from -128 to -33
- level_high: int32 [1], replicated, may hold values from 32 to 127
Outputs:
- input_grads: bfloat16 [1024, 14848], P('col', 'row')
- weight_grads: bfloat16 [14848, 29696], P('row', 'col')
- step_grads: float32 [29696], P('col')
The draws below stay inside these ranges and needn't reach their ends.
Inputs may be any that keep to these rules, and one draw needn't show every extreme that they name: `step_sizes`: every step size is one of the five powers of two 2^-13, 2^-12, 2^-11, 2^-10, 2^-9, each taken by about a fifth of the channels.
All inputs are finite; a program needn't handle non-finite values.
Results may differ from the reference program's by a relative error of at most 0.017.
Values may be sent and summed in bfloat16 or wider, within the bound.
No kernel may reach another device: no remote copies, remote signals or barrier semaphores. Data moves between devices by JAX's collectives and lax.ppermute only.
A program may use at most 64 MiB of HBM per device.

```python
import jax
import jax.numpy as jnp
from jax import lax

D = 14848
F = 29696
TOKENS = 1024
N_COL = 16


def draw_step_sizes(key, part):
    key = jax.random.fold_in(key, 7)
    table = jnp.array([2.0 ** (-13), 2.0 ** (-12), 2.0 ** (-11), 2.0 ** (-10), 2.0 ** (-9)], jnp.float32)
    picks = jax.random.permutation(key, F) % 5
    return jnp.take(table, picks.astype(jnp.int32)).astype(jnp.float32)


def strengthened(drawn, rng, source, target, blocks, factor):
    def block_of(dim):
        return (jnp.arange(drawn.shape[dim]) // (drawn.shape[dim] // blocks)).reshape((-1,) + (1,) * (drawn.ndim - 1 - dim))

    first = jax.random.permutation(rng, blocks)[block_of(target)]
    other_side = (block_of(target) + blocks // 2) % blocks
    return jnp.where((block_of(source) == first) | (block_of(source) == other_side), factor * drawn, drawn)


def block_levels(key, shape, split, smallest, high):
    level, own = 1.0, jax.random.fold_in(key, 6)
    for dim, shards_of in split:
        steps = jnp.exp(jax.random.uniform(jax.random.fold_in(own, dim), (shards_of,), jnp.float32, smallest / len(split), high / len(split)))
        level = level * jnp.repeat(steps, shape[dim] // shards_of).reshape([-1 if axis == dim else 1 for axis in range(len(shape))])
    return level


def centred(own_key, extent, scale, limit, split=(), held_as=jnp.bfloat16):
    values = jax.random.normal(own_key, extent, jnp.float32) * scale
    if len(split) > 0:
        values = block_levels(own_key, extent, split, -0.22, 0.18) * values
    return jnp.clip(values, min=-limit, max=limit).astype(held_as)


def noise_with(stream_key, shape, scale, reach, shards, heavy, kind=jnp.bfloat16):
    result = scale * jax.random.normal(stream_key, shape, jnp.float32)
    if shards:
        result = result * block_levels(stream_key, shape, shards, -0.22, 0.18)
    return jnp.clip(strengthened(result, jax.random.fold_in(stream_key, 3), *heavy), -reach, reach).astype(kind)


def setup_inputs(seed: int = 0) -> dict:
    key_of = jax.random.split(jax.random.key(seed), 7)
    activations = centred(key_of[0], (TOKENS, D), 1.0, 6.0, ((0, 16), (1, 32)))
    output_grads = noise_with(key_of[1], (TOKENS, F), 0.125, 1.0, ((0, 32), (1, 16)), (1, 0, 32, 2.75))
    weight = centred(key_of[2], (D, F), D ** -0.5, 0.046875, ((0, 32), (1, 16)))
    step_sizes = draw_step_sizes(jax.random.fold_in(key_of[6], 71), 0)
    level_low = jax.random.randint(key_of[4], (1,), -128, -32).astype(jnp.int32)
    level_high = jax.random.randint(key_of[5], (1,), 32, 128).astype(jnp.int32)
    return dict(activations=activations, output_grads=output_grads, weight=weight, step_sizes=step_sizes, level_low=level_low, level_high=level_high)


def quantize(weight, steps, low, high):
    ratio = weight.astype(jnp.float32) / steps[None, :]
    levels = jnp.clip(jnp.floor(ratio + 0.5), low, high)
    inside = jnp.logical_and(ratio >= low, ratio <= high)
    quantized = (levels * steps[None, :]).astype(jnp.bfloat16)
    coefficient = jnp.where(inside, levels - ratio, levels)
    return (quantized, inside.astype(jnp.float32), coefficient)

def reference(activations, output_grads, weight, step_sizes, level_low, level_high):
    low = level_low[0].astype(jnp.float32)
    high = level_high[0].astype(jnp.float32)
    scale = 1.0 / jnp.sqrt(jnp.float32(D) * high)
    width = F // N_COL

    def block(total, index):
        start = (index * width).astype(jnp.int32)
        wblock = lax.dynamic_slice_in_dim(weight, start, width, 1)
        sblock = lax.dynamic_slice_in_dim(step_sizes, start, width, 0)
        gblock = lax.dynamic_slice_in_dim(output_grads, start, width, 1)
        quantized, inside, coefficient = quantize(wblock, sblock, low, high)
        wgrad = lax.dot_general(activations, gblock, (((0,), (0,)), ((), ())), preferred_element_type=jnp.float32)
        partial_sum = lax.dot_general(gblock, quantized, (((1,), (1,)), ((), ())), preferred_element_type=jnp.float32)
        rounded = lax.optimization_barrier(partial_sum.astype(jnp.bfloat16))
        total = total + rounded.astype(jnp.float32)
        sgrad = lax.optimization_barrier(jnp.sum(wgrad * coefficient, axis=0)) * scale
        return (total, ((wgrad * inside).astype(jnp.bfloat16), sgrad))
    start_total = jnp.zeros((TOKENS, D), jnp.float32)
    total, (wblocks, sblocks) = lax.scan(block, start_total, jnp.arange(N_COL, dtype=jnp.int32))
    weight_grads = jnp.transpose(wblocks, (1, 0, 2)).reshape(D, F)
    return (total.astype(jnp.bfloat16), weight_grads, sblocks.reshape(F))
```

```python
import jax
import jax.numpy as jnp
from jax import lax
from jax.sharding import Mesh, PartitionSpec as P

ROW = ("y", "zl", "c")
COL = ("zh", "x")


def quantize(weight, steps, low, high):
    ratio = weight.astype(jnp.float32) / steps[None, :]
    levels = jnp.clip(jnp.floor(ratio + 0.5), low, high)
    inside = jnp.logical_and(ratio >= low, ratio <= high)
    quantized = (levels * steps[None, :]).astype(jnp.bfloat16)
    coefficient = jnp.where(inside, levels - ratio, levels)
    return (quantized, inside.astype(jnp.float32), coefficient)


def shards(activations, output_grads, weight, step_sizes, level_low, level_high):
    f32, bf16 = jnp.float32, jnp.bfloat16
    low = level_low[0].astype(f32)
    high = level_high[0].astype(f32)
    quantized, inside, coefficient = quantize(weight, step_sizes, low, high)
    features, channels = weight.shape
    core = lax.axis_index("c")

    act = activations.reshape(2, 32, features)
    act = jnp.where(core == 0, act, act[::-1])
    act = lax.all_gather(act, "zh", axis=0)
    act = lax.all_gather(act, "x", axis=0)

    grads = lax.all_gather(output_grads, "zl", axis=0)
    pieces = []
    for p in range(2):
        own = lax.all_gather(grads[2 * p : 2 * p + 2], "y", axis=0)
        other = lax.ppermute(own, "c", [(0, 1), (1, 0)])
        pieces += [own, other]
    grads = jnp.stack(pieces).reshape(2, 2, 4, 2, 32, channels)
    rows = grads.reshape(1024, channels)
    act = act.reshape(2, 2, 4, 2, 32, features).transpose(0, 3, 2, 1, 4, 5).reshape(1024, features)

    partial_rows = lax.dot_general(
        rows, quantized, (((1,), (1,)), ((), ())), preferred_element_type=f32
    ).astype(bf16)
    sums = partial_rows.reshape(2, 2, 4, 2, 32, features).transpose(0, 3, 2, 1, 4, 5)
    sums = sums.reshape(4, 4, 64, features)
    sums = lax.all_to_all(sums, "x", 0, 0)
    sums = jnp.sum(sums.astype(f32), axis=0).astype(bf16)
    sums = lax.all_to_all(sums, "zh", 0, 0)
    sums = jnp.sum(sums.astype(f32), axis=0).astype(bf16).reshape(2, 32, features)
    input_grads = jnp.where(core == 0, sums, sums[::-1]).reshape(64, features)

    wgrad = lax.dot_general(act, rows, (((0,), (0,)), ((), ())), preferred_element_type=f32)
    weight_grads = (wgrad * inside).astype(bf16)
    local = jnp.sum(wgrad * coefficient, axis=0)
    scale = 1.0 / jnp.sqrt(f32(features * 32) * high)
    total = lax.psum(lax.psum(lax.psum(local, "c"), "zl"), "y")
    return (input_grads, weight_grads, total * scale)


def solution(mesh):
    fine = Mesh(mesh.devices.reshape(4, 4, 2, 4, 4), ROW + COL)
    placed = (P(COL, ROW), P(ROW, COL), P(ROW, COL), P(COL), P(), P())
    return jax.shard_map(
        shards,
        mesh=fine,
        in_specs=placed,
        out_specs=(P(COL, ROW), P(ROW, COL), P(COL)),
        check_vma=False,
    )
```

```python
import jax
import jax.numpy as jnp
from jax import lax
from jax.sharding import Mesh, PartitionSpec as P

ROW = ("y", "zl", "c")
COL = ("zh", "x")
SWAP = [(0, 1), (1, 0)]


def quantize(weight, steps, low, high):
    ratio = weight.astype(jnp.float32) / steps[None, :]
    levels = jnp.clip(jnp.floor(ratio + 0.5), low, high)
    inside = jnp.logical_and(ratio >= low, ratio <= high)
    quantized = (levels * steps[None, :]).astype(jnp.bfloat16)
    coefficient = jnp.where(inside, levels - ratio, levels)
    return (quantized, inside.astype(jnp.float32), coefficient)


def gather(block, axis):
    return lax.all_to_all(jnp.broadcast_to(block[None], (4, *block.shape)), axis, 0, 0)


def shards(activations, output_grads, weight, step_sizes, level_low, level_high):
    f32, bf16 = jnp.float32, jnp.bfloat16
    low = level_low[0].astype(f32)
    high = level_high[0].astype(f32)
    quantized, inside, coefficient = quantize(weight, step_sizes, low, high)
    features, channels = weight.shape
    core = lax.axis_index("c")

    grads = lax.all_gather(output_grads, "zl", axis=0)
    activations, grads = lax.optimization_barrier((activations, grads))
    grads = grads.reshape(4, 2, 16, channels)
    own = [gather(grads[:, h], "y") for h in range(2)]

    act = activations.reshape(2, 32, features)
    act = jnp.where(core == 0, act, act[::-1])
    act = gather(gather(act, "zh"), "x")
    act = act.reshape(4, 4, 2, 2, 16, features).transpose(3, 2, 1, 0, 4, 5)
    act = act.reshape(1024, features)

    rows, sums = [], []
    for h in range(2):
        both = jnp.concatenate([own[h], lax.ppermute(own[h], "c", SWAP)]).reshape(512, channels)
        rows.append(both)
        part = lax.dot_general(
            both, quantized, (((1,), (1,)), ((), ())), preferred_element_type=f32
        ).astype(bf16)
        part = part.reshape(2, 4, 4, 16, features).transpose(2, 1, 0, 3, 4)
        part = lax.all_to_all(part, "x", 0, 0)
        sums.append(jnp.sum(part.astype(f32), axis=0).astype(bf16))
    sums = lax.all_to_all(jnp.stack(sums, axis=2), "zh", 0, 0)
    sums = jnp.sum(sums.astype(f32), axis=0).astype(bf16).reshape(2, 32, features)
    input_grads = jnp.where(core == 0, sums, sums[::-1]).reshape(64, features)

    wgrad = lax.dot_general(
        act, jnp.concatenate(rows), (((0,), (0,)), ((), ())), preferred_element_type=f32
    )
    weight_grads = (wgrad * inside).astype(bf16)
    local = jnp.sum(wgrad * coefficient, axis=0)
    scale = 1.0 / jnp.sqrt(f32(features * 32) * high)
    total = lax.psum(lax.psum(lax.psum(local, "c"), "y"), "zl")
    return (input_grads, weight_grads, total * scale)


def solution(mesh):
    fine = Mesh(mesh.devices.reshape(4, 4, 2, 4, 4), ROW + COL)
    placed = (P(COL, ROW), P(ROW, COL), P(ROW, COL), P(COL), P(), P())
    return jax.shard_map(
        shards,
        mesh=fine,
        in_specs=placed,
        out_specs=(P(COL, ROW), P(ROW, COL), P(COL)),
        check_vma=False,
    )
```

```python
import jax
import jax.numpy as jnp
from jax import lax
from jax.experimental import pallas as pl
from jax.experimental.pallas import tpu as pltpu
from jax.sharding import Mesh, PartitionSpec as P

ROW = ("y", "zl", "c")
COL = ("zh", "x")
SWAP = [(0, 1), (1, 0)]
TILE = 512
tie = lax.optimization_barrier
SMEM = pl.BlockSpec(memory_space=pltpu.SMEM)
VMEM = pl.BlockSpec(memory_space=pltpu.VMEM)
CONTRACT_LAST = (((1,), (1,)), ((), ()))
CONTRACT_FIRST = (((0,), (0,)), ((), ()))


def own_rows_kernel(bounds, own, w, steps, quantized, out):
    step = steps[...]
    ratio = w[...].astype(jnp.float32) * (1.0 / step)
    levels = jnp.clip(jnp.floor(ratio + 0.5), bounds[0], bounds[1])
    quantized[...] = (levels * step).astype(jnp.bfloat16)
    rows = own[...].reshape(512, own.shape[-1])
    out[...] = lax.dot_general(
        rows, quantized[...], CONTRACT_LAST, preferred_element_type=jnp.float32
    ).astype(jnp.bfloat16)


def own_rows(bounds, own, weight, steps):
    features, channels = weight.shape
    return pl.pallas_call(
        own_rows_kernel,
        out_shape=(
            jax.ShapeDtypeStruct(weight.shape, jnp.bfloat16),
            jax.ShapeDtypeStruct((512, features), jnp.bfloat16),
        ),
        in_specs=[SMEM, VMEM, VMEM, VMEM],
        out_specs=(VMEM, VMEM),
        compiler_params=pltpu.CompilerParams(vmem_limit_bytes=60 << 20),
        cost_estimate=pl.CostEstimate(
            flops=2 * 512 * features * channels,
            bytes_accessed=2 * (2 * features * channels + 512 * (features + channels)),
            transcendentals=0,
        ),
    )(bounds, own, weight, steps)


def all_rows_kernel(place, mine, other, quantized, out):
    rows = other[...].reshape(512, other.shape[-1])
    part = lax.dot_general(
        rows, quantized[...], CONTRACT_LAST, preferred_element_type=jnp.float32
    ).astype(jnp.bfloat16)
    core = place[1]
    at_mine = pl.multiple_of(core * 32, 32)
    at_other = pl.multiple_of((1 - core) * 32, 32)
    for y in range(4):
        for z in range(4):
            at = 32 * (4 * y + z)
            out[z, y, pl.ds(at_mine, 32), :] = mine[at : at + 32, :]
            out[z, y, pl.ds(at_other, 32), :] = part[at : at + 32]


def all_rows(place, mine, other, quantized):
    features, channels = quantized.shape
    return pl.pallas_call(
        all_rows_kernel,
        out_shape=jax.ShapeDtypeStruct((4, 4, 64, features), jnp.bfloat16),
        in_specs=[SMEM, VMEM, VMEM, VMEM],
        out_specs=VMEM,
        compiler_params=pltpu.CompilerParams(vmem_limit_bytes=60 << 20),
        cost_estimate=pl.CostEstimate(
            flops=2 * 512 * features * channels,
            bytes_accessed=2 * (features * channels + 512 * (4 * features + channels)),
            transcendentals=0,
        ),
    )(place, mine, other, quantized)


def weight_kernel(place, bounds, act, own, other, w, steps, out, sums, rows):
    core = place[1]

    @pl.when(pl.program_id(0) == 0)
    def _():
        for o in range(2):
            start = pl.multiple_of(jnp.abs(o - core) * 32, 32)
            for y in range(4):
                for z in range(4):
                    at = 512 * o + 32 * (4 * y + z)
                    rows[at : at + 32, :] = act[z, y, pl.ds(start, 32), :]

    grads = jnp.concatenate([own[...].reshape(512, TILE), other[...].reshape(512, TILE)], axis=0)
    wgrad = lax.dot_general(rows[...], grads, CONTRACT_FIRST, preferred_element_type=jnp.float32)
    low, high = bounds[0], bounds[1]
    ratio = w[...].astype(jnp.float32) * (1.0 / steps[...])
    levels = jnp.clip(jnp.floor(ratio + 0.5), low, high)
    inside = jnp.logical_and(ratio >= low, ratio <= high)
    out[...] = jnp.where(inside, wgrad, 0.0).astype(jnp.bfloat16)
    coefficient = jnp.where(inside, levels - ratio, levels)
    sums[...] = jnp.sum(wgrad * coefficient, axis=0, keepdims=True)


def weight_and_step_sums(place, bounds, act, own, other, weight, steps):
    features, channels = weight.shape
    column = lambda rows: pl.BlockSpec((rows, TILE), lambda j: (0, j))
    block = pl.BlockSpec((4, 4, 32, TILE), lambda j: (0, 0, 0, j))
    return pl.pallas_call(
        weight_kernel,
        grid=(pl.cdiv(channels, TILE),),
        out_shape=(
            jax.ShapeDtypeStruct(weight.shape, jnp.bfloat16),
            jax.ShapeDtypeStruct((1, channels), jnp.float32),
        ),
        in_specs=[SMEM, SMEM, pl.BlockSpec(act.shape, lambda j: (0, 0, 0, 0)), block, block]
        + [column(features), column(1)],
        out_specs=(column(features), column(1)),
        scratch_shapes=[pltpu.VMEM((1024, features), jnp.bfloat16)],
        compiler_params=pltpu.CompilerParams(vmem_limit_bytes=60 << 20),
        cost_estimate=pl.CostEstimate(
            flops=2 * 1024 * features * channels,
            bytes_accessed=2 * (2 * features * channels + 1024 * (features + channels)),
            transcendentals=0,
        ),
    )(place, bounds, act, own, other, weight, steps)


def gather(block, axis):
    return lax.all_to_all(jnp.broadcast_to(block[None], (4, *block.shape)), axis, 0, 0)


def shards(activations, output_grads, weight, step_sizes, level_low, level_high):
    f32, bf16 = jnp.float32, jnp.bfloat16
    features, channels = weight.shape
    high = level_high[0].astype(f32)
    bounds = jnp.stack([level_low[0].astype(f32), high])
    steps = step_sizes[None, :]
    place = jnp.stack([lax.axis_index(a) for a in ("y", "c", "zh", "x")]).astype(jnp.int32)

    grads = gather(output_grads, "zl")
    grads, activations = tie((grads, activations))

    own = gather(grads, "y")
    act = lax.all_gather(activations, "zh", axis=0)
    own, act = tie((own, act))

    act = gather(act, "x")
    other = lax.ppermute(own, "c", SWAP)
    quantized, mine = own_rows(bounds, own, weight, steps)
    sums = all_rows(place, mine, other, quantized)
    sums, act = tie((sums, act))

    sums = lax.all_to_all(sums, "x", 0, 0)
    sums = jnp.sum(sums.astype(f32), axis=0).astype(bf16)
    weight_grads, local = weight_and_step_sums(place, bounds, act, own, other, weight, steps)
    total = lax.psum(lax.psum(local[0], "c"), "zl")
    sums, total, weight_grads = tie((sums, total, weight_grads))

    sums = lax.all_to_all(sums, "zh", 0, 0)
    input_grads = jnp.sum(sums.astype(f32), axis=0).astype(bf16)
    scale = 1.0 / jnp.sqrt(f32(features * 32) * high)
    total = lax.psum(total, "y")
    return (input_grads, weight_grads, total * scale)


def solution(mesh):
    fine = Mesh(mesh.devices.reshape(4, 4, 2, 4, 4), ROW + COL)
    placed = (P(COL, ROW), P(ROW, COL), P(ROW, COL), P(COL), P(), P())
    return jax.shard_map(
        shards,
        mesh=fine,
        in_specs=placed,
        out_specs=(P(COL, ROW), P(ROW, COL), P(COL)),
        check_vma=False,
    )
```

```python
import jax
import jax.numpy as jnp
from jax import lax
from jax.experimental import pallas as pl
from jax.experimental.pallas import tpu as pltpu
from jax.sharding import Mesh, PartitionSpec as P

ROW = ("y", "zl", "c")
COL = ("zh", "x")
SWAP = [(0, 1), (1, 0)]
TILE = 512
HALVES = ((0, 256), (256, 464))
ANY = pl.BlockSpec(memory_space=pl.ANY)
SMEM = pl.BlockSpec(memory_space=pltpu.SMEM)
VMEM = pl.BlockSpec(memory_space=pltpu.VMEM)
CONTRACT_LAST = (((1,), (1,)), ((), ()))
tie = lax.optimization_barrier


def resident(array):
    return pltpu.with_memory_space_constraint(array, pltpu.VMEM)


def distant(array):
    return pltpu.with_memory_space_constraint(array, pltpu.HBM)


def quantize_kernel(low, high, w, steps, quantized):
    low, high = low[0].astype(jnp.float32), high[0].astype(jnp.float32)
    step = steps[...][None, :]
    ratio = w[...].astype(jnp.float32) * (1.0 / step)
    levels = jnp.clip(jnp.floor(ratio + 0.5), low, high)
    quantized[...] = (levels * step).astype(jnp.bfloat16)


def quantize(low, high, weight, steps):
    features, channels = weight.shape
    return pl.pallas_call(
        quantize_kernel,
        out_shape=pltpu.HBM(weight.shape, jnp.bfloat16),
        in_specs=[SMEM, SMEM, VMEM, VMEM],
        out_specs=VMEM,
        compiler_params=pltpu.CompilerParams(vmem_limit_bytes=24 << 20),
        cost_estimate=pl.CostEstimate(
            flops=10 * features * channels, bytes_accessed=4 * features * channels, transcendentals=0
        ),
    )(low, high, weight, steps)


def products_kernel(
    low, high, own, other, act, quantized_hbm, w_hbm, steps, sums_hbm, grads_hbm, local,
    quantized, w, rows, sums, grads, sems,
):
    core = lax.axis_index("c")
    at_own = pl.multiple_of(core * 32, 32)
    at_other = pl.multiple_of((1 - core) * 32, 32)
    parts = [pl.ds(top, bottom - top) for top, bottom in HALVES]
    loads = [
        pltpu.make_async_copy(quantized_hbm.at[part], quantized.at[part], sems.at[n])
        for n, part in enumerate(parts)
    ]
    loads.append(pltpu.make_async_copy(w_hbm, w, sems.at[2]))
    for load in loads:
        load.start()
    low, high = low[0].astype(jnp.float32), high[0].astype(jnp.float32)
    features, channels = w.shape
    tiles = [(a, min(a + TILE, channels)) for a in range(0, channels, TILE)]

    for (top, bottom), load in zip(HALVES, loads[:2]):
        load.wait()
        for tokens, at in ((own, at_own), (other, at_other)):
            part = lax.dot_general(
                tokens[...].reshape(512, channels),
                quantized[top:bottom, :],
                CONTRACT_LAST,
                preferred_element_type=jnp.float32,
            ).astype(jnp.bfloat16)
            for y in range(4):
                for z in range(4):
                    sums[z, y, pl.ds(at, 32), top:bottom] = part[32 * (4 * y + z) : 32 * (4 * y + z) + 32]
    stores = [pltpu.make_async_copy(sums, sums_hbm, sems.at[3])]
    stores[0].start()

    for z in range(4):
        tokens = [act[z, y, pl.ds(at, 32), :] for y in range(4) for at in (at_own, at_other)]
        rows[:, 256 * z : 256 * z + 256] = jnp.concatenate(tokens, axis=0).T

    loads[2].wait()
    scale = 1.0 / jnp.sqrt(jnp.full((1, 128), 32 * features * high, jnp.float32))
    for n, (top, bottom) in enumerate(HALVES):
        for a, b in tiles:
            blocks = [half[4 * y + z, :, a:b] for z in range(4) for y in range(4) for half in (own, other)]
            wgrad = jnp.dot(rows[top:bottom, :], jnp.concatenate(blocks, axis=0), preferred_element_type=jnp.float32)
            ratio = w[top:bottom, a:b].astype(jnp.float32) * (1.0 / steps[a:b][None, :])
            levels = jnp.clip(jnp.floor(ratio + 0.5), low, high)
            inside = jnp.logical_and(ratio >= low, ratio <= high)
            grads[top:bottom, a:b] = jnp.where(inside, wgrad, 0.0).astype(jnp.bfloat16)
            coefficient = jnp.where(inside, levels - ratio, levels)
            partial = jnp.sum(wgrad * coefficient, axis=0) * scale[0, 0]
            local[a:b] = partial if n == 0 else local[a:b] + partial
        stores.append(pltpu.make_async_copy(grads.at[parts[n]], grads_hbm.at[parts[n]], sems.at[4 + n]))
        stores[-1].start()
    for store in stores:
        store.wait()


def products(low, high, own, other, act, quantized, weight, steps):
    features, channels = weight.shape
    own, other = (tokens.reshape(16, 32, channels) for tokens in (own, other))
    bf16 = jnp.bfloat16
    return pl.pallas_call(
        products_kernel,
        out_shape=(
            pltpu.HBM((4, 4, 64, features), bf16),
            pltpu.HBM(weight.shape, bf16),
            jax.ShapeDtypeStruct((channels,), jnp.float32),
        ),
        in_specs=[SMEM, SMEM, VMEM, VMEM, VMEM, ANY, ANY, VMEM],
        out_specs=(ANY, ANY, VMEM),
        scratch_shapes=[
            pltpu.VMEM(weight.shape, bf16),
            pltpu.VMEM(weight.shape, bf16),
            pltpu.VMEM((features, 1024), bf16),
            pltpu.VMEM((4, 4, 64, features), bf16),
            pltpu.VMEM(weight.shape, bf16),
            pltpu.SemaphoreType.DMA((6,)),
        ],
        compiler_params=pltpu.CompilerParams(vmem_limit_bytes=24 << 20),
        cost_estimate=pl.CostEstimate(
            flops=4 * 1024 * features * channels,
            bytes_accessed=2 * (2 * features * channels + 1024 * (2 * features + channels)),
            transcendentals=0,
        ),
    )(low, high, *map(resident, (own, other, act)), distant(quantized), distant(weight), steps)


def gather(block, axis):
    return lax.all_to_all(jnp.broadcast_to(block[None], (4, *block.shape)), axis, 0, 0)


def shards(activations, output_grads, weight, step_sizes, level_low, level_high):
    f32, bf16 = jnp.float32, jnp.bfloat16

    grads = gather(output_grads, "zl")
    act = lax.all_gather(activations, "zh", axis=0)
    grads, act = tie((grads, act))

    own = gather(grads, "y")
    act = lax.all_gather(act, "x", axis=0)
    quantized = quantize(level_low, level_high, weight, step_sizes)
    own, act, quantized = tie((own, act, quantized))

    other = lax.ppermute(own, "c", SWAP)
    sums, weight_grads, total = products(level_low, level_high, own, other, act, quantized, weight, step_sizes)

    sums = lax.all_to_all(sums, "x", 0, 0)
    sums = jnp.sum(sums.astype(f32), axis=0).astype(bf16)
    total = lax.psum(lax.psum(total, "c"), "zl")
    sums, total = tie((sums, total))

    sums = lax.all_to_all(sums, "zh", 0, 0)
    input_grads = jnp.sum(sums.astype(f32), axis=0).astype(bf16)
    return (input_grads, weight_grads, lax.psum(total, "y"))


def solution(mesh):
    fine = Mesh(mesh.devices.reshape(4, 4, 2, 4, 4), ROW + COL)
    placed = (P(COL, ROW), P(ROW, COL), P(ROW, COL), P(COL), P(), P())
    return jax.shard_map(
        shards,
        mesh=fine,
        in_specs=placed,
        out_specs=(P(COL, ROW), P(ROW, COL), P(COL)),
        check_vma=False,
    )
```

```python
import jax
import jax.numpy as jnp
from jax import lax
from jax.experimental import pallas as pl
from jax.experimental.pallas import tpu as pltpu
from jax.sharding import Mesh, PartitionSpec as P

ROW = ("y", "zl", "c")
COL = ("zh", "x")
SWAP = [(0, 1), (1, 0)]
TILE = 512
HALVES = ((0, 256), (256, 464))
ANY = pl.BlockSpec(memory_space=pl.ANY)
SMEM = pl.BlockSpec(memory_space=pltpu.SMEM)
VMEM = pl.BlockSpec(memory_space=pltpu.VMEM)
CONTRACT_LAST = (((1,), (1,)), ((), ()))
tie = lax.optimization_barrier


def resident(array):
    return pltpu.with_memory_space_constraint(array, pltpu.VMEM)


def distant(array):
    return pltpu.with_memory_space_constraint(array, pltpu.HBM)


def products_kernel(
    bounds, own, other, act, w_hbm, steps, sums_hbm, grads_hbm, local,
    quantized, w, rows, sums, grads, sems,
):
    core = lax.axis_index("c")
    at_own = pl.multiple_of(core * 32, 32)
    at_other = pl.multiple_of((1 - core) * 32, 32)
    parts = [pl.ds(top, bottom - top) for top, bottom in HALVES]
    loads = [pltpu.make_async_copy(w_hbm.at[part], w.at[part], sems.at[n]) for n, part in enumerate(parts)]
    for load in loads:
        load.start()
    low, high = bounds[0], bounds[1]
    features, channels = w.shape
    tiles = [(a, min(a + TILE, channels)) for a in range(0, channels, TILE)]

    for (top, bottom), load in zip(HALVES, loads):
        load.wait()
        for a, b in tiles:
            step = steps[a:b][None, :]
            ratio = w[top:bottom, a:b].astype(jnp.float32) * (1.0 / step)
            levels = jnp.clip(jnp.floor(ratio + 0.5), low, high)
            quantized[top:bottom, a:b] = (levels * step).astype(jnp.bfloat16)
        for tokens, at in ((own, at_own), (other, at_other)):
            part = lax.dot_general(
                tokens[...].reshape(512, channels),
                quantized[top:bottom, :],
                CONTRACT_LAST,
                preferred_element_type=jnp.float32,
            ).astype(jnp.bfloat16)
            for y in range(4):
                for z in range(4):
                    sums[z, y, pl.ds(at, 32), top:bottom] = part[32 * (4 * y + z) : 32 * (4 * y + z) + 32]
    stores = [pltpu.make_async_copy(sums, sums_hbm, sems.at[2])]
    stores[0].start()

    for z in range(4):
        tokens = [act[z, y, pl.ds(at, 32), :] for y in range(4) for at in (at_own, at_other)]
        rows[:, 256 * z : 256 * z + 256] = jnp.concatenate(tokens, axis=0).T

    scale = 1.0 / jnp.sqrt(jnp.full((1, 128), 32 * features * high, jnp.float32))
    for n, (top, bottom) in enumerate(HALVES):
        for a, b in tiles:
            blocks = [half[4 * y + z, :, a:b] for z in range(4) for y in range(4) for half in (own, other)]
            wgrad = jnp.dot(rows[top:bottom, :], jnp.concatenate(blocks, axis=0), preferred_element_type=jnp.float32)
            ratio = w[top:bottom, a:b].astype(jnp.float32) * (1.0 / steps[a:b][None, :])
            levels = jnp.clip(jnp.floor(ratio + 0.5), low, high)
            inside = jnp.logical_and(ratio >= low, ratio <= high)
            grads[top:bottom, a:b] = jnp.where(inside, wgrad, 0.0).astype(jnp.bfloat16)
            coefficient = jnp.where(inside, levels - ratio, levels)
            partial = jnp.sum(wgrad * coefficient, axis=0) * scale[0, 0]
            local[a:b] = partial if n == 0 else local[a:b] + partial
        stores.append(pltpu.make_async_copy(grads.at[parts[n]], grads_hbm.at[parts[n]], sems.at[3 + n]))
        stores[-1].start()
    for store in stores:
        store.wait()


def products(bounds, own, other, act, weight, steps):
    features, channels = weight.shape
    own, other = (tokens.reshape(16, 32, channels) for tokens in (own, other))
    bf16 = jnp.bfloat16
    return pl.pallas_call(
        products_kernel,
        out_shape=(
            pltpu.HBM((4, 4, 64, features), bf16),
            pltpu.HBM(weight.shape, bf16),
            jax.ShapeDtypeStruct((channels,), jnp.float32),
        ),
        in_specs=[SMEM, VMEM, VMEM, VMEM, ANY, VMEM],
        out_specs=(ANY, ANY, VMEM),
        scratch_shapes=[
            pltpu.VMEM(weight.shape, bf16),
            pltpu.VMEM(weight.shape, bf16),
            pltpu.VMEM((features, 1024), bf16),
            pltpu.VMEM((4, 4, 64, features), bf16),
            pltpu.VMEM(weight.shape, bf16),
            pltpu.SemaphoreType.DMA((5,)),
        ],
        compiler_params=pltpu.CompilerParams(vmem_limit_bytes=24 << 20),
        cost_estimate=pl.CostEstimate(
            flops=4 * 1024 * features * channels,
            bytes_accessed=2 * (2 * features * channels + 1024 * (2 * features + channels)),
            transcendentals=0,
        ),
    )(bounds, *map(resident, (own, other, act)), distant(weight), steps)


def gather(block, axis):
    return lax.all_to_all(jnp.broadcast_to(block[None], (4, *block.shape)), axis, 0, 0)


def shards(activations, output_grads, weight, step_sizes, level_low, level_high):
    f32, bf16 = jnp.float32, jnp.bfloat16

    grads = gather(output_grads, "zl")
    grads, activations = tie((grads, activations))

    own = gather(grads, "y")
    act = lax.all_gather(activations, "zh", axis=0)
    bounds = jnp.concatenate([level_low, level_high]).astype(f32)
    own, act, bounds = tie((own, act, bounds))

    other = lax.ppermute(own, "c", SWAP)
    act = lax.all_gather(act, "x", axis=0)
    sums, weight_grads, total = products(bounds, own, other, act, weight, step_sizes)

    sums = lax.all_to_all(sums, "x", 0, 0)
    sums = jnp.sum(sums.astype(f32), axis=0).astype(bf16)
    total = lax.psum(total, "zl")
    sums, total = tie((sums, total))

    sums = lax.all_to_all(sums, "zh", 0, 0)
    input_grads = jnp.sum(sums.astype(f32), axis=0).astype(bf16)
    return (input_grads, weight_grads, lax.psum(lax.psum(total, "y"), "c"))


def solution(mesh):
    fine = Mesh(mesh.devices.reshape(4, 4, 2, 4, 4), ROW + COL)
    placed = (P(COL, ROW), P(ROW, COL), P(ROW, COL), P(COL), P(), P())
    return jax.shard_map(
        shards,
        mesh=fine,
        in_specs=placed,
        out_specs=(P(COL, ROW), P(ROW, COL), P(COL)),
        check_vma=False,
    )
```

```python
import jax
import jax.numpy as jnp
from jax import lax
from jax.experimental import pallas as pl
from jax.experimental.pallas import tpu as pltpu
from jax.sharding import Mesh, PartitionSpec as P

ROW = ("y", "zl", "c")
COL = ("zh", "x")
SWAP = [(0, 1), (1, 0)]
TILE = 512
HALVES = ((0, 256), (256, 464))
ANY = pl.BlockSpec(memory_space=pl.ANY)
SMEM = pl.BlockSpec(memory_space=pltpu.SMEM)
VMEM = pl.BlockSpec(memory_space=pltpu.VMEM)
CONTRACT_LAST = (((1,), (1,)), ((), ()))
tie = lax.optimization_barrier


def resident(array):
    return pltpu.with_memory_space_constraint(array, pltpu.VMEM)


def distant(array):
    return pltpu.with_memory_space_constraint(array, pltpu.HBM)


def products_kernel(
    bounds, own, other, act, w_hbm, steps, sums_hbm, grads_hbm, local,
    quantized, w, rows, sums, grads, sems,
):
    core = lax.axis_index("c")
    at_own = pl.multiple_of(core * 32, 32)
    at_other = pl.multiple_of((1 - core) * 32, 32)
    parts = [pl.ds(top, bottom - top) for top, bottom in HALVES]
    loads = [pltpu.make_async_copy(w_hbm.at[part], w.at[part], sems.at[n]) for n, part in enumerate(parts)]
    for load in loads:
        load.start()
    low, high = bounds[0], bounds[1]
    features, channels = w.shape
    tiles = [(a, min(a + TILE, channels)) for a in range(0, channels, TILE)]

    for z in range(4):
        tokens = [act[z, y, pl.ds(at, 32), :] for y in range(4) for at in (at_own, at_other)]
        rows[:, 256 * z : 256 * z + 256] = jnp.concatenate(tokens, axis=0).T

    for (top, bottom), load in zip(HALVES, loads):
        load.wait()
        for a, b in tiles:
            step = steps[a:b][None, :]
            ratio = w[top:bottom, a:b].astype(jnp.float32) * (1.0 / step)
            levels = jnp.clip(jnp.floor(ratio + 0.5), low, high)
            quantized[top:bottom, a:b] = (levels * step).astype(jnp.bfloat16)
        for tokens, at in ((own, at_own), (other, at_other)):
            part = lax.dot_general(
                tokens[...].reshape(512, channels),
                quantized[top:bottom, :],
                CONTRACT_LAST,
                preferred_element_type=jnp.float32,
            ).astype(jnp.bfloat16)
            for y in range(4):
                for z in range(4):
                    sums[z, y, pl.ds(at, 32), top:bottom] = part[32 * (4 * y + z) : 32 * (4 * y + z) + 32]
    stores = [pltpu.make_async_copy(sums, sums_hbm, sems.at[2])]
    stores[0].start()

    scale = 1.0 / jnp.sqrt(jnp.full((1, 128), 32 * features * high, jnp.float32))
    for n, (top, bottom) in enumerate(HALVES):
        for a, b in tiles:
            blocks = [half[4 * y + z, :, a:b] for z in range(4) for y in range(4) for half in (own, other)]
            wgrad = jnp.dot(rows[top:bottom, :], jnp.concatenate(blocks, axis=0), preferred_element_type=jnp.float32)
            ratio = w[top:bottom, a:b].astype(jnp.float32) * (1.0 / steps[a:b][None, :])
            levels = jnp.clip(jnp.floor(ratio + 0.5), low, high)
            inside = jnp.logical_and(ratio >= low, ratio <= high)
            grads[top:bottom, a:b] = jnp.where(inside, wgrad, 0.0).astype(jnp.bfloat16)
            coefficient = jnp.where(inside, levels - ratio, levels)
            partial = jnp.sum(wgrad * coefficient, axis=0) * scale[0, 0]
            local[a:b] = partial if n == 0 else local[a:b] + partial
        stores.append(pltpu.make_async_copy(grads.at[parts[n]], grads_hbm.at[parts[n]], sems.at[3 + n]))
        stores[-1].start()
    for store in stores:
        store.wait()


def products(bounds, own, other, act, weight, steps):
    features, channels = weight.shape
    own, other = (tokens.reshape(16, 32, channels) for tokens in (own, other))
    bf16 = jnp.bfloat16
    return pl.pallas_call(
        products_kernel,
        out_shape=(
            pltpu.HBM((4, 4, 64, features), bf16),
            pltpu.HBM(weight.shape, bf16),
            jax.ShapeDtypeStruct((channels,), jnp.float32),
        ),
        in_specs=[SMEM, VMEM, VMEM, VMEM, ANY, VMEM],
        out_specs=(ANY, ANY, VMEM),
        scratch_shapes=[
            pltpu.VMEM(weight.shape, bf16),
            pltpu.VMEM(weight.shape, bf16),
            pltpu.VMEM((features, 1024), bf16),
            pltpu.VMEM((4, 4, 64, features), bf16),
            pltpu.VMEM(weight.shape, bf16),
            pltpu.SemaphoreType.DMA((5,)),
        ],
        compiler_params=pltpu.CompilerParams(vmem_limit_bytes=24 << 20),
        cost_estimate=pl.CostEstimate(
            flops=4 * 1024 * features * channels,
            bytes_accessed=2 * (2 * features * channels + 1024 * (2 * features + channels)),
            transcendentals=0,
        ),
    )(pltpu.with_memory_space_constraint(bounds, pltpu.SMEM), *map(resident, (own, other, act)), distant(weight), steps)


def gather(block, axis):
    return lax.all_to_all(jnp.broadcast_to(block[None], (4, *block.shape)), axis, 0, 0)


def shards(activations, output_grads, weight, step_sizes, level_low, level_high):
    f32, bf16 = jnp.float32, jnp.bfloat16

    grads = lax.all_gather(output_grads, "zl", axis=0)
    grads, activations = tie((grads, activations))

    own = gather(grads, "y")
    act = lax.all_gather(activations, "zh", axis=0)
    bounds = jnp.concatenate([level_low, level_high]).astype(f32)
    own, act, bounds = tie((own, act, bounds))

    other = lax.ppermute(own, "c", SWAP)
    act = lax.all_gather(act, "x", axis=0)
    sums, weight_grads, total = products(bounds, own, other, act, weight, step_sizes)

    sums = lax.all_to_all(sums, "x", 0, 0)
    sums = jnp.sum(sums.astype(f32), axis=0).astype(bf16)
    total = lax.psum(total, "zl")
    sums, total = tie((sums, total))

    sums = lax.all_to_all(sums, "zh", 0, 0)
    input_grads = jnp.sum(sums.astype(f32), axis=0).astype(bf16)
    return (input_grads, weight_grads, lax.psum(lax.psum(total, "y"), "c"))


def solution(mesh):
    fine = Mesh(mesh.devices.reshape(4, 4, 2, 4, 4), ROW + COL)
    placed = (P(COL, ROW), P(ROW, COL), P(ROW, COL), P(COL), P(), P())
    return jax.shard_map(
        shards,
        mesh=fine,
        in_specs=placed,
        out_specs=(P(COL, ROW), P(ROW, COL), P(COL)),
        check_vma=False,
    )
```

```python
import jax
import jax.numpy as jnp
from jax import lax
from jax.experimental import pallas as pl
from jax.experimental.pallas import tpu as pltpu
from jax.sharding import Mesh, PartitionSpec as P

ROW = ("y", "zl", "c")
COL = ("zh", "x")
SWAP = [(0, 1), (1, 0)]
TILE = 512
HALVES = ((0, 256), (256, 464))
ANY = pl.BlockSpec(memory_space=pl.ANY)
SMEM = pl.BlockSpec(memory_space=pltpu.SMEM)
VMEM = pl.BlockSpec(memory_space=pltpu.VMEM)
CONTRACT_LAST = (((1,), (1,)), ((), ()))
tie = lax.optimization_barrier


def resident(array):
    return pltpu.with_memory_space_constraint(array, pltpu.VMEM)


def distant(array):
    return pltpu.with_memory_space_constraint(array, pltpu.HBM)


def products_kernel(
    bounds, own, other, act, w_hbm, steps, sums_hbm, grads_hbm, local,
    quantized, w, rows, sums, grads, sems,
):
    core = lax.axis_index("c")
    at_own = pl.multiple_of(core * 32, 32)
    at_other = pl.multiple_of((1 - core) * 32, 32)
    parts = [pl.ds(top, bottom - top) for top, bottom in HALVES]
    loads = [pltpu.make_async_copy(w_hbm.at[part], w.at[part], sems.at[n]) for n, part in enumerate(parts)]
    for load in loads:
        load.start()
    low, high = bounds[0], bounds[1]
    features, channels = w.shape
    tiles = [(a, min(a + TILE, channels)) for a in range(0, channels, TILE)]

    for z in range(4):
        tokens = [act[z, y, pl.ds(at, 32), :] for y in range(4) for at in (at_own, at_other)]
        rows[:, 256 * z : 256 * z + 256] = jnp.concatenate(tokens, axis=0).T

    for (top, bottom), load in zip(HALVES, loads):
        load.wait()
        for a, b in tiles:
            step = steps[a:b][None, :]
            ratio = w[top:bottom, a:b].astype(jnp.float32) * (1.0 / step)
            levels = jnp.clip(jnp.floor(ratio + 0.5), low, high)
            quantized[top:bottom, a:b] = (levels * step).astype(jnp.bfloat16)
        for tokens, at in ((own, at_own), (other, at_other)):
            part = lax.dot_general(
                tokens[...].reshape(512, channels),
                quantized[top:bottom, :],
                CONTRACT_LAST,
                preferred_element_type=jnp.float32,
            ).astype(jnp.bfloat16)
            for y in range(4):
                for z in range(4):
                    sums[z, y, pl.ds(at, 32), top:bottom] = part[32 * (4 * y + z) : 32 * (4 * y + z) + 32]
    stores = [pltpu.make_async_copy(sums, sums_hbm, sems.at[2])]
    stores[0].start()

    scale = 1.0 / jnp.sqrt(jnp.full((1, 128), 32 * features * high, jnp.float32))
    for n, (top, bottom) in enumerate(HALVES):
        for a, b in tiles:
            blocks = [half[4 * y + z, :, a:b] for z in range(4) for y in range(4) for half in (own, other)]
            wgrad = jnp.dot(rows[top:bottom, :], jnp.concatenate(blocks, axis=0), preferred_element_type=jnp.float32)
            ratio = w[top:bottom, a:b].astype(jnp.float32) * (1.0 / steps[a:b][None, :])
            levels = jnp.clip(jnp.floor(ratio + 0.5), low, high)
            inside = jnp.logical_and(ratio >= low, ratio <= high)
            grads[top:bottom, a:b] = jnp.where(inside, wgrad, 0.0).astype(jnp.bfloat16)
            coefficient = jnp.where(inside, levels - ratio, levels)
            partial = jnp.sum(wgrad * coefficient, axis=0) * scale[0, 0]
            local[a:b] = partial if n == 0 else local[a:b] + partial
        stores.append(pltpu.make_async_copy(grads.at[parts[n]], grads_hbm.at[parts[n]], sems.at[3 + n]))
        stores[-1].start()
    for store in stores:
        store.wait()


def products(bounds, own, other, act, weight, steps):
    features, channels = weight.shape
    own, other = (tokens.reshape(16, 32, channels) for tokens in (own, other))
    bf16 = jnp.bfloat16
    return pl.pallas_call(
        products_kernel,
        out_shape=(
            pltpu.HBM((4, 4, 64, features), bf16),
            pltpu.HBM(weight.shape, bf16),
            jax.ShapeDtypeStruct((channels,), jnp.float32),
        ),
        in_specs=[SMEM, VMEM, VMEM, VMEM, ANY, VMEM],
        out_specs=(ANY, ANY, VMEM),
        scratch_shapes=[
            pltpu.VMEM(weight.shape, bf16),
            pltpu.VMEM(weight.shape, bf16),
            pltpu.VMEM((features, 1024), bf16),
            pltpu.VMEM((4, 4, 64, features), bf16),
            pltpu.VMEM(weight.shape, bf16),
            pltpu.SemaphoreType.DMA((5,)),
        ],
        compiler_params=pltpu.CompilerParams(vmem_limit_bytes=24 << 20),
        cost_estimate=pl.CostEstimate(
            flops=4 * 1024 * features * channels,
            bytes_accessed=2 * (2 * features * channels + 1024 * (2 * features + channels)),
            transcendentals=0,
        ),
    )(pltpu.with_memory_space_constraint(bounds, pltpu.SMEM), *map(resident, (own, other, act)), distant(weight), steps)


def gather(block, axis):
    return lax.all_to_all(jnp.broadcast_to(block[None], (4, *block.shape)), axis, 0, 0)


def shards(activations, output_grads, weight, step_sizes, level_low, level_high):
    f32, bf16 = jnp.float32, jnp.bfloat16

    grads = lax.all_gather(output_grads, "zl", axis=0)
    grads, activations = tie((grads, activations))

    own = gather(grads, "y")
    act = lax.all_gather(activations, "zh", axis=0)
    bounds = jnp.concatenate([level_low, level_high]).astype(f32)
    own, act, bounds = tie((own, act, bounds))

    other = lax.ppermute(own, "c", SWAP)
    act = lax.all_gather(act, "x", axis=0)
    sums, weight_grads, total = products(bounds, own, other, act, weight, step_sizes)

    sums = lax.all_to_all(sums, "x", 0, 0)
    sums = jnp.sum(sums.astype(f32), axis=0).astype(bf16)
    total = lax.psum(total, "zl")
    sums, total = tie((sums, total))

    sums = lax.all_to_all(sums, "zh", 0, 0)
    input_grads = jnp.sum(sums.astype(f32), axis=0).astype(bf16)
    return (input_grads, weight_grads, lax.psum(lax.psum(total, "c"), "y"))


def solution(mesh):
    fine = Mesh(mesh.devices.reshape(4, 4, 2, 4, 4), ROW + COL)
    placed = (P(COL, ROW), P(ROW, COL), P(ROW, COL), P(COL), P(), P())
    return jax.shard_map(
        shards,
        mesh=fine,
        in_specs=placed,
        out_specs=(P(COL, ROW), P(ROW, COL), P(COL)),
        check_vma=False,
    )
```
